32 devices in a mesh: dp: 16 (over z, y, x), clus: 2 (over core).
Axes of the slice: x: 2, y: 2, z: 4, core: 2. Of those that a mesh axis runs over, the one named last changes fastest.
Arguments:
- embeddings: bfloat16 [8192, 4096], P('dp'), may hold values from -6 to 6
- assignment: int32 [8192], P('dp'), may hold values from 0 to 95
- slot_of: int32 [96], replicated, may hold values from 0 to 95, each once
- old_centroids: bfloat16 [96, 4096], P(('clus', 'dp')), may hold values from -6 to 6
Outputs:
- new_centroids: float32 [96, 4096], P(('clus', 'dp'))
- distance: float32 [8192], P('dp')
The draws below stay inside these ranges and needn't reach their ends.
All inputs are finite; a program needn't handle non-finite values.
Results may differ from the reference program's by a relative error of at most 0.0003.
Values may be sent and summed in bfloat16 or wider, within the bound.
A program may use at most 64 MiB of HBM per device.

```python
import math
import jax
import jax.numpy as jnp
import numpy as np
from jax import lax

D = 4096
TOK_DEV = 512
POINTS = 8192
CLUSTERS = 96
N_DP = 16


def place_ends(values, rng, smallest, top_value):
    longest = values.shape.index(max(values.shape))
    spots = []
    for shift in (0, 1):
        where = [jax.random.randint(jax.random.fold_in(rng, axis), (), 0, length) for axis, length in enumerate(values.shape)]
        where[longest] = (where[longest] + shift) % values.shape[longest]
        spots.append(tuple(where))
    return values.at[spots[0]].set(smallest).at[spots[1]].set(top_value)


def block_scale(own_key, dims, cuts, least, largest):
    def one(dim, parts):
        draws = jax.random.uniform(jax.random.fold_in(jax.random.fold_in(own_key, 6), dim), (parts,), jnp.float32, least / len(cuts), largest / len(cuts))
        return jnp.repeat(jnp.exp(draws), dims[dim] // parts).reshape((-1,) + (1,) * (len(dims) - dim - 1))

    factor_of = one(*cuts[0])
    for cut in cuts[1:]:
        factor_of = factor_of * one(*cut)
    return factor_of


def rank_table(number_of, skew):
    loads = [(1 << 20) // math.isqrt(standing ** skew) + 1 for standing in range(1, number_of + 1)]
    width = 1 + sum(loads) // (1 << 30)
    return np.cumsum(np.array([max(1, weight // width) for weight in loads]))


def ranked(key, dims, number_of, lean):
    listing = rank_table(number_of, lean)
    lot = jax.random.randint(jax.random.fold_in(key, 1), dims, 0, int(listing[number_of - 1]))
    rank = jnp.searchsorted(jnp.asarray(listing, jnp.int32), lot, side="right")
    return jax.random.permutation(jax.random.fold_in(key, 2), number_of)[rank].astype(jnp.int32)


def normal_values(stream_key, extent, width, limit, split=(), dtype=jnp.bfloat16):
    level = block_scale(stream_key, extent, split, -0.22, 0.18) if split else 1.0
    values = jax.random.normal(stream_key, extent, jnp.float32) * width * level
    return jnp.minimum(jnp.maximum(values, -limit), limit).astype(dtype)


def setup_inputs(seed: int = 0) -> dict:
    key_of = jax.random.split(jax.random.key(seed), 5)
    return {
        "embeddings": normal_values(key_of[0], (POINTS, D), 1.0, 6.0, ((0, 16),)),
        "assignment": place_ends(ranked(key_of[1], (POINTS,), CLUSTERS, 2), jax.random.fold_in(key_of[1], 3), 0, CLUSTERS - 1).astype(jnp.int32),
        "slot_of": jax.random.permutation(key_of[2], CLUSTERS).astype(jnp.int32),
        "old_centroids": normal_values(key_of[3], (CLUSTERS, D), 1.0, 6.0, ((0, 32),)),
    }


def reference(embeddings, assignment, slot_of, old_centroids):
    clusters = old_centroids.shape[0]
    slot_ids = slot_of[assignment].astype(jnp.int32)
    points = embeddings.reshape(N_DP, TOK_DEV, D)
    slots = slot_ids.reshape(N_DP, TOK_DEV)
    cent_wide = old_centroids.astype(jnp.float32)
    cent_rms = jnp.sqrt(lax.optimization_barrier(jnp.mean(cent_wide * cent_wide, axis=1)) + 1e-06)

    def step(totals, inputs):
        rows, row_slots = inputs
        rows_wide = rows.astype(jnp.float32)
        totals = totals + jax.ops.segment_sum(rows_wide, row_slots, clusters)
        picked = old_centroids[row_slots].astype(jnp.float32)
        scores = lax.optimization_barrier(jnp.sum(rows_wide * picked, axis=1))
        root_mean = jnp.sqrt(lax.optimization_barrier(jnp.mean(rows_wide * rows_wide, axis=1)) + 1e-06)
        return (totals, 1.0 - scores / (jnp.float32(D) * root_mean * cent_rms[row_slots]))
    sums, distance = lax.scan(step, jnp.zeros((clusters, D), jnp.float32), (points, slots))
    overall = sums + cent_wide
    updated = overall * lax.rsqrt(lax.optimization_barrier(jnp.mean(overall * overall, axis=1, keepdims=True)) + 1e-06)
    return (updated, distance.reshape(-1))
```

```python
import functools

import jax
import jax.numpy as jnp
from jax import lax
from jax.experimental import pallas as pl
from jax.experimental.pallas import tpu as pltpu
from jax.sharding import PartitionSpec as P

LANES = 128
EPS = 1e-06


def inner_size(n):
    g = 1
    while n % (g * 2) == 0 and (g * 2) * (g * 2) <= n:
        g *= 2
    return g


def kernel(
    n, g, n_clus, nc,
    emb_hbm, asg_ref, slot_ref, cent_ref, new_ref, dist_ref,
    emb, sums, recv1, part, recv2, fin, cent_own, cent, cent_wide, cent_mat, sq, mine, theirs,
    emb_sem, s1_send, s1_recv, s2_send, s2_recv, g1_send, g1_recv, g2_send, g2_recv, x_send, x_recv,
):
    big = n // g
    rows, width = cent_ref.shape
    points = emb.shape[0]
    clusters = slot_ref.shape[1]
    block = n * rows
    tiles = width // LANES
    kc = tiles // nc
    cw = kc * LANES
    me = lax.axis_index("dp")
    own_clus = lax.axis_index("clus")
    zo, p = me // g, me % g

    def device(dp):
        return {"dp": dp}

    loads = []
    for c in range(nc):
        cols = pl.ds(c * cw, cw)
        cp = pltpu.make_async_copy(emb_hbm.at[:, cols], emb.at[:, cols], emb_sem.at[c])
        cp.start()
        loads.append(cp)

    inner = [zo * g + lax.rem(p + j, g) for j in range(1, g)]
    outer = [lax.rem(zo + i, big) * g + p for i in range(1, big)]
    partners = [lax.rem(own_clus + q, n_clus) for q in range(1, n_clus)]

    barrier = pltpu.get_barrier_semaphore()
    for d in inner + outer:
        pl.semaphore_signal(barrier, inc=1, device_id=device(d), device_id_type=pl.DeviceIdType.MESH)
    for q in partners:
        pl.semaphore_signal(barrier, inc=1, device_id={"clus": q}, device_id_type=pl.DeviceIdType.MESH)

    def remote(src, dst, send, recv, where):
        cp = pltpu.make_async_remote_copy(
            src_ref=src, dst_ref=dst, send_sem=send, recv_sem=recv,
            device_id=where, device_id_type=pl.DeviceIdType.MESH,
        )
        cp.start()
        return cp

    old = cent_ref[...].astype(jnp.float32)
    for k in range(tiles):
        cent_own[pl.ds(k, rows, stride=tiles), :] = old[:, k * LANES:(k + 1) * LANES]
    cent[p, zo] = cent_own[...].astype(jnp.bfloat16)

    j = lax.broadcasted_iota(jnp.int32, (block, clusters), 0)
    local = ((j // rows) % big * g + j // (rows * big)) * rows + j % rows
    place = (slot_ref[...] == local + own_clus * block).astype(jnp.float32).astype(jnp.bfloat16)
    which = (
        lax.broadcasted_iota(jnp.int32, (clusters, points), 0) == asg_ref[...]
    ).astype(jnp.float32).astype(jnp.bfloat16)
    hot_wide = jnp.dot(place, which, preferred_element_type=jnp.float32)
    hot = hot_wide.astype(jnp.bfloat16)

    pl.semaphore_wait(barrier, len(inner) + len(outer) + len(partners))

    started = []
    gather1 = [
        remote(cent.at[p, zo], cent.at[p, zo], g1_send.at[i], g1_recv.at[i], device(d))
        for i, d in enumerate(outer)
    ]

    span = big * rows * kc
    step1 = []
    for c in range(nc):
        loads[c].wait()
        value = jnp.dot(hot, emb[:, c * cw:(c + 1) * cw], preferred_element_type=jnp.float32)
        for k in range(kc):
            sums[pl.ds(c * block * kc + k, block, stride=kc), :] = value[:, k * LANES:(k + 1) * LANES]
        copies = []
        for i, d in enumerate(inner):
            start = pl.multiple_of(c * block * kc + lax.rem(p + i + 1, g) * span, 8)
            copies.append(
                remote(sums.at[pl.ds(start, span)], recv1.at[c, i], s1_send.at[c, i], s1_recv.at[c, i], device(d))
            )
        step1.append(copies)
        x = emb[:, c * cw:(c + 1) * cw].astype(jnp.float32)
        x = x * x
        acc = x[:, :LANES]
        for k in range(1, kc):
            acc = acc + x[:, k * LANES:(k + 1) * LANES]
        if c == 0:
            sq[...] = acc
        else:
            sq[...] += acc

    for cp in gather1:
        cp.wait_recv()
    gather2 = [
        remote(cent.at[p], cent.at[p], g2_send.at[i], g2_recv.at[i], device(d))
        for i, d in enumerate(inner)
    ]

    sub = rows * kc
    step2 = []
    for c in range(nc):
        for cp in step1[c]:
            cp.wait_recv()
        start = pl.multiple_of(c * block * kc + p * span, 8)
        total = sums[pl.ds(start, span), :]
        for i in range(g - 1):
            total = total + recv1[c, i]
        part[c] = total.reshape(big, sub, LANES)
        step2.append([
            remote(
                part.at[c, lax.rem(zo + i + 1, big)], recv2.at[c, i],
                s2_send.at[c, i], s2_recv.at[c, i], device(d),
            )
            for i, d in enumerate(outer)
        ])

    ones = jnp.ones((8, LANES), jnp.float32)
    sumsq = lax.dot_general(
        ones, sq[...], (((1,), (1,)), ((), ())),
        preferred_element_type=jnp.float32, precision=lax.Precision.HIGHEST,
    )[:1]
    root_mean = jnp.sqrt(sumsq / width + EPS)

    for cp in gather2:
        cp.wait_recv()
    wide = cent[...].astype(jnp.float32).reshape(block * tiles, LANES)
    cent_wide[...] = wide
    cent_sq = jnp.sum(
        jnp.sum((wide * wide).reshape(block, tiles, LANES), axis=1), axis=1, keepdims=True
    )
    cent_rms = jnp.sqrt(cent_sq / width + EPS)
    for k in range(tiles):
        cent_mat[:, k * LANES:(k + 1) * LANES] = cent_wide[
            pl.ds(k, block, stride=tiles), :
        ].astype(jnp.bfloat16)
    raw = lax.dot_general(
        cent_mat[...], emb[...], (((1,), (1,)), ((), ())), preferred_element_type=jnp.float32
    )
    picked = jnp.sum(hot_wide * (raw / cent_rms), axis=0, keepdims=True)
    share = picked / (jnp.float32(width) * root_mean)
    mine[...] = jnp.broadcast_to(share, mine.shape)
    swap = [
        remote(mine, theirs.at[i], x_send.at[i], x_recv.at[i], {"clus": q})
        for i, q in enumerate(partners)
    ]

    for c in range(nc):
        for cp in step2[c]:
            cp.wait_recv()
        total = part[c, zo]
        for i in range(big - 1):
            total = total + recv2[c, i]
        fin[pl.ds(c * sub, sub), :] = total
    for c in range(nc):
        for k in range(kc):
            t = (c * kc + k) * LANES
            new_ref[:, t:t + LANES] = fin[pl.ds(c * sub + k, rows, stride=kc), :] + old[:, t:t + LANES]
    overall = new_ref[...]
    new_ref[...] = overall * lax.rsqrt(jnp.mean(overall * overall, axis=1, keepdims=True) + EPS)

    score = mine[:1]
    for i, cp in enumerate(swap):
        cp.wait_recv()
        score = score + theirs[i, :1]
    dist_ref[...] = 1.0 - score

    for cp in gather1 + gather2 + swap + sum(step1, []) + sum(step2, []):
        cp.wait_send()


def per_device(n, n_clus, embeddings, assignment, slot_of, old_centroids):
    points, width = embeddings.shape
    rows = old_centroids.shape[0]
    clusters = slot_of.shape[0]
    g = inner_size(n)
    big = n // g
    block = n * rows
    tiles = width // LANES
    nc = 4
    kc = tiles // nc
    dma = pltpu.SemaphoreType.DMA
    vmem = pl.BlockSpec(memory_space=pltpu.VMEM)
    new, dist = pl.pallas_call(
        functools.partial(kernel, n, g, n_clus, nc),
        out_shape=(
            jax.ShapeDtypeStruct((rows, width), jnp.float32),
            jax.ShapeDtypeStruct((1, points), jnp.float32),
        ),
        in_specs=[pl.BlockSpec(memory_space=pl.ANY), vmem, vmem, vmem],
        out_specs=(vmem, vmem),
        scratch_shapes=[
            pltpu.VMEM((points, width), embeddings.dtype),
            pltpu.VMEM((block * tiles, LANES), jnp.float32),
            pltpu.VMEM((nc, g - 1, big * rows * kc, LANES), jnp.float32),
            pltpu.VMEM((nc, big, rows * kc, LANES), jnp.float32),
            pltpu.VMEM((nc, big - 1, rows * kc, LANES), jnp.float32),
            pltpu.VMEM((rows * tiles, LANES), jnp.float32),
            pltpu.VMEM((rows * tiles, LANES), jnp.float32),
            pltpu.VMEM((g, big, rows * tiles, LANES), jnp.bfloat16),
            pltpu.VMEM((block * tiles, LANES), jnp.float32),
            pltpu.VMEM((block, width), jnp.bfloat16),
            pltpu.VMEM((points, LANES), jnp.float32),
            pltpu.VMEM((8, points), jnp.float32),
            pltpu.VMEM((n_clus - 1, 8, points), jnp.float32),
            dma((nc,)),
            dma((nc, g - 1)), dma((nc, g - 1)),
            dma((nc, big - 1)), dma((nc, big - 1)),
            dma((big - 1,)), dma((big - 1,)),
            dma((g - 1,)), dma((g - 1,)),
            dma((n_clus - 1,)), dma((n_clus - 1,)),
        ],
        compiler_params=pltpu.CompilerParams(
            collective_id=0, has_side_effects=True, vmem_limit_bytes=48 * 1024 * 1024
        ),
    )(embeddings, assignment.reshape(1, points), slot_of.reshape(1, clusters), old_centroids)
    return new, dist.reshape(points)


def solution(mesh):
    in_specs = (P("dp", None), P("dp"), P(), P(("clus", "dp"), None))
    out_specs = (P(("clus", "dp"), None), P("dp"))
    return jax.shard_map(
        functools.partial(per_device, mesh.shape["dp"], mesh.shape["clus"]),
        mesh=mesh, in_specs=in_specs, out_specs=out_specs, check_vma=False,
    )
```

```python
import functools

import jax
import jax.numpy as jnp
from jax import lax
from jax.experimental import pallas as pl
from jax.experimental.pallas import tpu as pltpu
from jax.sharding import PartitionSpec as P

LANES = 128
EPS = 1e-06
VMEM_BYTES = 64 * 1024 * 1024


def inner_size(n):
    g = 1
    while n % (g * 2) == 0 and (g * 2) * (g * 2) <= n:
        g *= 2
    return g


def kernel(
    n, g, n_clus, nc,
    emb_hbm, asg_hbm, slot_hbm, cent_hbm, new_ref, dist_ref,
    asg_ref, slot_ref, cent_ref, emb, sums, recv1, part, recv2, fin, cent_own, cent, cent_wide, cent_mat, sq, mine, theirs,
    in_sem, emb_sem, s1_send, s1_recv, s2_send, s2_recv, g1_send, g1_recv, g2_send, g2_recv, x_send, x_recv,
):
    big = n // g
    rows, width = cent_ref.shape
    points = emb.shape[0]
    clusters = slot_ref.shape[1]
    block = n * rows
    tiles = width // LANES
    kc = tiles // nc
    cw = kc * LANES
    me = lax.axis_index("dp")
    own_clus = lax.axis_index("clus")
    zo, p = me // g, me % g

    def device(dp):
        return {"dp": dp}

    small = []
    for i, (src, dst) in enumerate(((cent_hbm, cent_ref), (slot_hbm, slot_ref), (asg_hbm, asg_ref))):
        cp = pltpu.make_async_copy(src, dst, in_sem.at[i])
        cp.start()
        small.append(cp)
    loads = []
    for c in range(nc):
        cols = pl.ds(c * cw, cw)
        cp = pltpu.make_async_copy(emb_hbm.at[:, cols], emb.at[:, cols], emb_sem.at[c])
        cp.start()
        loads.append(cp)

    inner = [zo * g + lax.rem(p + j, g) for j in range(1, g)]
    outer = [lax.rem(zo + i, big) * g + p for i in range(1, big)]
    partners = [lax.rem(own_clus + q, n_clus) for q in range(1, n_clus)]

    barrier = pltpu.get_barrier_semaphore()
    for d in inner + outer:
        pl.semaphore_signal(barrier, inc=1, device_id=device(d), device_id_type=pl.DeviceIdType.MESH)
    for q in partners:
        pl.semaphore_signal(barrier, inc=1, device_id={"clus": q}, device_id_type=pl.DeviceIdType.MESH)

    def remote(src, dst, send, recv, where):
        cp = pltpu.make_async_remote_copy(
            src_ref=src, dst_ref=dst, send_sem=send, recv_sem=recv,
            device_id=where, device_id_type=pl.DeviceIdType.MESH,
        )
        cp.start()
        return cp

    for cp in small:
        cp.wait()
    old = cent_ref[...].astype(jnp.float32)
    for k in range(tiles):
        cent_own[pl.ds(k, rows, stride=tiles), :] = old[:, k * LANES:(k + 1) * LANES]
    cent[p, zo] = cent_own[...].astype(jnp.bfloat16)

    j = lax.broadcasted_iota(jnp.int32, (block, clusters), 0)
    local = ((j // rows) % big * g + j // (rows * big)) * rows + j % rows
    place = (slot_ref[...] == local + own_clus * block).astype(jnp.float32).astype(jnp.bfloat16)
    which = (
        lax.broadcasted_iota(jnp.int32, (clusters, points), 0) == asg_ref[...]
    ).astype(jnp.float32).astype(jnp.bfloat16)
    hot_wide = jnp.dot(place, which, preferred_element_type=jnp.float32)
    hot = hot_wide.astype(jnp.bfloat16)

    span = big * rows * kc

    def block_sums(c):
        loads[c].wait()
        value = jnp.dot(hot, emb[:, c * cw:(c + 1) * cw], preferred_element_type=jnp.float32)
        for k in range(kc):
            sums[pl.ds(c * block * kc + k, block, stride=kc), :] = value[:, k * LANES:(k + 1) * LANES]

    def send_sums(c):
        copies = []
        for i, d in enumerate(inner):
            start = pl.multiple_of(c * block * kc + lax.rem(p + i + 1, g) * span, 8)
            copies.append(
                remote(sums.at[pl.ds(start, span)], recv1.at[c, i], s1_send.at[c, i], s1_recv.at[c, i], device(d))
            )
        return copies

    early = nc // 2
    for c in range(early):
        block_sums(c)

    pl.semaphore_wait(barrier, len(inner) + len(outer) + len(partners))

    gather1 = [
        remote(cent.at[p, zo], cent.at[p, zo], g1_send.at[i], g1_recv.at[i], device(d))
        for i, d in enumerate(outer)
    ]
    step1 = [send_sums(c) for c in range(early)]
    for c in range(early, nc):
        block_sums(c)
        step1.append(send_sums(c))

    for c in range(nc):
        x = emb[:, c * cw:(c + 1) * cw].astype(jnp.float32)
        x = x * x
        acc = x[:, :LANES]
        for k in range(1, kc):
            acc = acc + x[:, k * LANES:(k + 1) * LANES]
        if c == 0:
            sq[...] = acc
        else:
            sq[...] += acc

    for cp in gather1:
        cp.wait_recv()
    gather2 = [
        remote(cent.at[p], cent.at[p], g2_send.at[i], g2_recv.at[i], device(d))
        for i, d in enumerate(inner)
    ]

    sub = rows * kc
    step2 = []
    for c in range(nc):
        for cp in step1[c]:
            cp.wait_recv()
        start = pl.multiple_of(c * block * kc + p * span, 8)
        total = sums[pl.ds(start, span), :]
        for i in range(g - 1):
            total = total + recv1[c, i]
        part[c] = total.reshape(big, sub, LANES)
        step2.append([
            remote(
                part.at[c, lax.rem(zo + i + 1, big)], recv2.at[c, i],
                s2_send.at[c, i], s2_recv.at[c, i], device(d),
            )
            for i, d in enumerate(outer)
        ])

    ones = jnp.ones((8, LANES), jnp.float32)
    sumsq = lax.dot_general(
        ones, sq[...], (((1,), (1,)), ((), ())),
        preferred_element_type=jnp.float32, precision=lax.Precision.HIGHEST,
    )[:1]
    root_mean = jnp.sqrt(sumsq / width + EPS)

    for cp in gather2:
        cp.wait_recv()
    wide = cent[...].astype(jnp.float32).reshape(block * tiles, LANES)
    cent_wide[...] = wide
    cent_sq = jnp.sum(
        jnp.sum((wide * wide).reshape(block, tiles, LANES), axis=1), axis=1, keepdims=True
    )
    cent_rms = jnp.sqrt(cent_sq / width + EPS)
    for k in range(tiles):
        cent_mat[:, k * LANES:(k + 1) * LANES] = cent_wide[
            pl.ds(k, block, stride=tiles), :
        ].astype(jnp.bfloat16)
    raw = lax.dot_general(
        cent_mat[...], emb[...], (((1,), (1,)), ((), ())), preferred_element_type=jnp.float32
    )
    picked = jnp.sum(hot_wide * (raw / cent_rms), axis=0, keepdims=True)
    share = picked / (jnp.float32(width) * root_mean)
    mine[...] = jnp.broadcast_to(share, mine.shape)
    swap = [
        remote(mine, theirs.at[i], x_send.at[i], x_recv.at[i], {"clus": q})
        for i, q in enumerate(partners)
    ]

    for c in range(nc):
        for cp in step2[c]:
            cp.wait_recv()
        total = part[c, zo]
        for i in range(big - 1):
            total = total + recv2[c, i]
        fin[pl.ds(c * sub, sub), :] = total
    for c in range(nc):
        for k in range(kc):
            t = (c * kc + k) * LANES
            new_ref[:, t:t + LANES] = fin[pl.ds(c * sub + k, rows, stride=kc), :] + old[:, t:t + LANES]
    overall = new_ref[...]
    new_ref[...] = overall * lax.rsqrt(jnp.mean(overall * overall, axis=1, keepdims=True) + EPS)

    score = mine[:1]
    for i, cp in enumerate(swap):
        cp.wait_recv()
        score = score + theirs[i, :1]
    dist_ref[...] = 1.0 - score

    for cp in gather1 + gather2 + swap + sum(step1, []) + sum(step2, []):
        cp.wait_send()


def per_device(n, n_clus, embeddings, assignment, slot_of, old_centroids):
    points, width = embeddings.shape
    rows = old_centroids.shape[0]
    clusters = slot_of.shape[0]
    g = inner_size(n)
    big = n // g
    block = n * rows
    tiles = width // LANES
    nc = 4
    kc = tiles // nc
    dma = pltpu.SemaphoreType.DMA
    vmem = pl.BlockSpec(memory_space=pltpu.VMEM)
    new, dist = pl.pallas_call(
        functools.partial(kernel, n, g, n_clus, nc),
        out_shape=(
            jax.ShapeDtypeStruct((rows, width), jnp.float32),
            jax.ShapeDtypeStruct((1, points), jnp.float32),
        ),
        in_specs=[pl.BlockSpec(memory_space=pltpu.HBM)] * 4,
        out_specs=(vmem, vmem),
        scratch_shapes=[
            pltpu.VMEM((1, points), jnp.int32),
            pltpu.VMEM((1, clusters), jnp.int32),
            pltpu.VMEM((rows, width), old_centroids.dtype),
            pltpu.VMEM((points, width), embeddings.dtype),
            pltpu.VMEM((block * tiles, LANES), jnp.float32),
            pltpu.VMEM((nc, g - 1, big * rows * kc, LANES), jnp.float32),
            pltpu.VMEM((nc, big, rows * kc, LANES), jnp.float32),
            pltpu.VMEM((nc, big - 1, rows * kc, LANES), jnp.float32),
            pltpu.VMEM((rows * tiles, LANES), jnp.float32),
            pltpu.VMEM((rows * tiles, LANES), jnp.float32),
            pltpu.VMEM((g, big, rows * tiles, LANES), jnp.bfloat16),
            pltpu.VMEM((block * tiles, LANES), jnp.float32),
            pltpu.VMEM((block, width), jnp.bfloat16),
            pltpu.VMEM((points, LANES), jnp.float32),
            pltpu.VMEM((8, points), jnp.float32),
            pltpu.VMEM((n_clus - 1, 8, points), jnp.float32),
            dma((3,)),
            dma((nc,)),
            dma((nc, g - 1)), dma((nc, g - 1)),
            dma((nc, big - 1)), dma((nc, big - 1)),
            dma((big - 1,)), dma((big - 1,)),
            dma((g - 1,)), dma((g - 1,)),
            dma((n_clus - 1,)), dma((n_clus - 1,)),
        ],
        compiler_params=pltpu.CompilerParams(
            collective_id=0, has_side_effects=True, vmem_limit_bytes=VMEM_BYTES
        ),
    )(embeddings, assignment.reshape(1, points), slot_of.reshape(1, clusters), old_centroids)
    return new, dist.reshape(points)


def solution(mesh):
    in_specs = (P("dp", None), P("dp"), P(), P(("clus", "dp"), None))
    out_specs = (P(("clus", "dp"), None), P("dp"))
    return jax.shard_map(
        functools.partial(per_device, mesh.shape["dp"], mesh.shape["clus"]),
        mesh=mesh, in_specs=in_specs, out_specs=out_specs, check_vma=False,
    )
```

```python
import functools

import jax
import jax.numpy as jnp
from jax import lax
from jax.experimental import pallas as pl
from jax.experimental.pallas import tpu as pltpu
from jax.sharding import PartitionSpec as P

LANES = 128
EPS = 1e-06
VMEM_BYTES = 64 * 1024 * 1024


def inner_size(n):
    g = 1
    while n % (g * 2) == 0 and (g * 2) * (g * 2) <= n:
        g *= 2
    return g


def kernel(
    n, g, n_clus, nc,
    emb_hbm, asg_hbm, slot_hbm, cent_hbm, new_ref, dist_ref,
    asg_ref, slot_ref, cent_ref, emb, sums, recv1, part, recv2, fin, cent_own, cent, cent_wide, cent_mat, sq, mine, theirs,
    in_sem, emb_sem, s1_send, s1_recv, s2_send, s2_recv, g1_send, g1_recv, g2_send, g2_recv, x_send, x_recv,
):
    big = n // g
    rows, width = cent_ref.shape
    points = emb.shape[0]
    clusters = slot_ref.shape[1]
    block = n * rows
    tiles = width // LANES
    kc = tiles // nc
    cw = kc * LANES
    me = lax.axis_index("dp")
    own_clus = lax.axis_index("clus")
    zo, p = me // g, me % g

    def device(dp):
        return {"dp": dp}

    small = []
    for i, (src, dst) in enumerate(((cent_hbm, cent_ref), (slot_hbm, slot_ref), (asg_hbm, asg_ref))):
        cp = pltpu.make_async_copy(src, dst, in_sem.at[i])
        cp.start()
        small.append(cp)
    loads = []
    for c in range(nc):
        cols = pl.ds(c * cw, cw)
        cp = pltpu.make_async_copy(emb_hbm.at[:, cols], emb.at[:, cols], emb_sem.at[c])
        cp.start()
        loads.append(cp)

    inner = [zo * g + lax.rem(p + j, g) for j in range(1, g)]
    outer = [lax.rem(zo + i, big) * g + p for i in range(1, big)]
    partners = [lax.rem(own_clus + q, n_clus) for q in range(1, n_clus)]

    barrier = pltpu.get_barrier_semaphore()
    for d in inner + outer:
        pl.semaphore_signal(barrier, inc=1, device_id=device(d), device_id_type=pl.DeviceIdType.MESH)
    for q in partners:
        pl.semaphore_signal(barrier, inc=1, device_id={"clus": q}, device_id_type=pl.DeviceIdType.MESH)

    def remote(src, dst, send, recv, where):
        cp = pltpu.make_async_remote_copy(
            src_ref=src, dst_ref=dst, send_sem=send, recv_sem=recv,
            device_id=where, device_id_type=pl.DeviceIdType.MESH,
        )
        cp.start()
        return cp

    for cp in small:
        cp.wait()
    old = cent_ref[...].astype(jnp.float32)
    for k in range(tiles):
        cent_own[pl.ds(k, rows, stride=tiles), :] = old[:, k * LANES:(k + 1) * LANES]
    cent[p, zo] = cent_own[...].astype(jnp.bfloat16)

    j = lax.broadcasted_iota(jnp.int32, (block, clusters), 0)
    local = ((j // rows) % big * g + j // (rows * big)) * rows + j % rows
    place = (slot_ref[...] == local + own_clus * block).astype(jnp.float32).astype(jnp.bfloat16)
    which = (
        lax.broadcasted_iota(jnp.int32, (clusters, points), 0) == asg_ref[...]
    ).astype(jnp.float32).astype(jnp.bfloat16)
    hot_wide = jnp.dot(place, which, preferred_element_type=jnp.float32)
    hot = hot_wide.astype(jnp.bfloat16)

    span = big * rows * kc

    def block_sums(c):
        loads[c].wait()
        value = jnp.dot(hot, emb[:, c * cw:(c + 1) * cw], preferred_element_type=jnp.float32)
        for k in range(kc):
            sums[pl.ds(c * block * kc + k, block, stride=kc), :] = value[:, k * LANES:(k + 1) * LANES]

    def send_sums(c):
        copies = []
        for i, d in enumerate(inner):
            start = pl.multiple_of(c * block * kc + lax.rem(p + i + 1, g) * span, 8)
            copies.append(
                remote(sums.at[pl.ds(start, span)], recv1.at[c, i], s1_send.at[c, i], s1_recv.at[c, i], device(d))
            )
        return copies

    early = nc // 2
    for c in range(early):
        block_sums(c)

    pl.semaphore_wait(barrier, len(inner) + len(outer) + len(partners))

    gather1 = [
        remote(cent.at[p, zo], cent.at[p, zo], g1_send.at[i], g1_recv.at[i], device(d))
        for i, d in enumerate(outer)
    ]
    step1 = [send_sums(c) for c in range(early)]
    for c in range(early, nc):
        block_sums(c)
        step1.append(send_sums(c))

    def add_squares(c):
        x = emb[:, c * cw:(c + 1) * cw].astype(jnp.float32)
        x = x * x
        acc = x[:, :LANES]
        for k in range(1, kc):
            acc = acc + x[:, k * LANES:(k + 1) * LANES]
        if c == 0:
            sq[...] = acc
        else:
            sq[...] += acc

    sub = rows * kc
    step2 = []
    for c in range(nc):
        if c == 1:
            for cp in gather1:
                cp.wait_recv()
            gather2 = [
                remote(cent.at[p], cent.at[p], g2_send.at[i], g2_recv.at[i], device(d))
                for i, d in enumerate(inner)
            ]
        add_squares(c)
        for cp in step1[c]:
            cp.wait_recv()
        start = pl.multiple_of(c * block * kc + p * span, 8)
        total = sums[pl.ds(start, span), :]
        for i in range(g - 1):
            total = total + recv1[c, i]
        part[c] = total.reshape(big, sub, LANES)
        step2.append([
            remote(
                part.at[c, lax.rem(zo + i + 1, big)], recv2.at[c, i],
                s2_send.at[c, i], s2_recv.at[c, i], device(d),
            )
            for i, d in enumerate(outer)
        ])

    ones = jnp.ones((8, LANES), jnp.float32)
    sumsq = lax.dot_general(
        ones, sq[...], (((1,), (1,)), ((), ())),
        preferred_element_type=jnp.float32, precision=lax.Precision.HIGHEST,
    )[:1]
    root_mean = jnp.sqrt(sumsq / width + EPS)

    for cp in gather2:
        cp.wait_recv()
    wide = cent[...].astype(jnp.float32).reshape(block * tiles, LANES)
    cent_wide[...] = wide
    cent_sq = jnp.sum(
        jnp.sum((wide * wide).reshape(block, tiles, LANES), axis=1), axis=1, keepdims=True
    )
    cent_rms = jnp.sqrt(cent_sq / width + EPS)
    for k in range(tiles):
        cent_mat[:, k * LANES:(k + 1) * LANES] = cent_wide[
            pl.ds(k, block, stride=tiles), :
        ].astype(jnp.bfloat16)
    raw = lax.dot_general(
        cent_mat[...], emb[...], (((1,), (1,)), ((), ())), preferred_element_type=jnp.float32
    )
    picked = jnp.sum(hot_wide * (raw / cent_rms), axis=0, keepdims=True)
    share = picked / (jnp.float32(width) * root_mean)
    mine[...] = jnp.broadcast_to(share, mine.shape)
    swap = [
        remote(mine, theirs.at[i], x_send.at[i], x_recv.at[i], {"clus": q})
        for i, q in enumerate(partners)
    ]

    for c in range(nc):
        for cp in step2[c]:
            cp.wait_recv()
        total = part[c, zo]
        for i in range(big - 1):
            total = total + recv2[c, i]
        fin[pl.ds(c * sub, sub), :] = total
    for c in range(nc):
        for k in range(kc):
            t = (c * kc + k) * LANES
            new_ref[:, t:t + LANES] = fin[pl.ds(c * sub + k, rows, stride=kc), :] + old[:, t:t + LANES]
    overall = new_ref[...]
    new_ref[...] = overall * lax.rsqrt(jnp.mean(overall * overall, axis=1, keepdims=True) + EPS)

    score = mine[:1]
    for i, cp in enumerate(swap):
        cp.wait_recv()
        score = score + theirs[i, :1]
    dist_ref[...] = 1.0 - score

    for cp in gather1 + gather2 + swap + sum(step1, []) + sum(step2, []):
        cp.wait_send()


def per_device(n, n_clus, embeddings, assignment, slot_of, old_centroids):
    points, width = embeddings.shape
    rows = old_centroids.shape[0]
    clusters = slot_of.shape[0]
    g = inner_size(n)
    big = n // g
    block = n * rows
    tiles = width // LANES
    nc = 2
    kc = tiles // nc
    dma = pltpu.SemaphoreType.DMA
    vmem = pl.BlockSpec(memory_space=pltpu.VMEM)
    new, dist = pl.pallas_call(
        functools.partial(kernel, n, g, n_clus, nc),
        out_shape=(
            jax.ShapeDtypeStruct((rows, width), jnp.float32),
            jax.ShapeDtypeStruct((1, points), jnp.float32),
        ),
        in_specs=[pl.BlockSpec(memory_space=pltpu.HBM)] * 4,
        out_specs=(vmem, vmem),
        scratch_shapes=[
            pltpu.VMEM((1, points), jnp.int32),
            pltpu.VMEM((1, clusters), jnp.int32),
            pltpu.VMEM((rows, width), old_centroids.dtype),
            pltpu.VMEM((points, width), embeddings.dtype),
            pltpu.VMEM((block * tiles, LANES), jnp.float32),
            pltpu.VMEM((nc, g - 1, big * rows * kc, LANES), jnp.float32),
            pltpu.VMEM((nc, big, rows * kc, LANES), jnp.float32),
            pltpu.VMEM((nc, big - 1, rows * kc, LANES), jnp.float32),
            pltpu.VMEM((rows * tiles, LANES), jnp.float32),
            pltpu.VMEM((rows * tiles, LANES), jnp.float32),
            pltpu.VMEM((g, big, rows * tiles, LANES), jnp.bfloat16),
            pltpu.VMEM((block * tiles, LANES), jnp.float32),
            pltpu.VMEM((block, width), jnp.bfloat16),
            pltpu.VMEM((points, LANES), jnp.float32),
            pltpu.VMEM((8, points), jnp.float32),
            pltpu.VMEM((n_clus - 1, 8, points), jnp.float32),
            dma((3,)),
            dma((nc,)),
            dma((nc, g - 1)), dma((nc, g - 1)),
            dma((nc, big - 1)), dma((nc, big - 1)),
            dma((big - 1,)), dma((big - 1,)),
            dma((g - 1,)), dma((g - 1,)),
            dma((n_clus - 1,)), dma((n_clus - 1,)),
        ],
        compiler_params=pltpu.CompilerParams(
            collective_id=0, has_side_effects=True, vmem_limit_bytes=VMEM_BYTES
        ),
    )(embeddings, assignment.reshape(1, points), slot_of.reshape(1, clusters), old_centroids)
    return new, dist.reshape(points)


def solution(mesh):
    in_specs = (P("dp", None), P("dp"), P(), P(("clus", "dp"), None))
    out_specs = (P(("clus", "dp"), None), P("dp"))
    return jax.shard_map(
        functools.partial(per_device, mesh.shape["dp"], mesh.shape["clus"]),
        mesh=mesh, in_specs=in_specs, out_specs=out_specs, check_vma=False,
    )
```
